768 devices in a mesh: index: 24 (over x, z_hi, core), ingest: 32 (over y, z_lo).
Axes of the slice: x: 4, y: 8, z: 12 (z_hi: 3, z_lo: 4; z = z_hi * 4 + z_lo), core: 2. Of those that a mesh axis runs over, the one named last changes fastest.
Arguments:
- vectors: bfloat16 [98304, 768], P(('index', 'ingest')), may hold values from -6 to 6
- rotation: bfloat16 [768, 768], replicated, may hold values from -0.21875 to 0.21875
- centroids: bfloat16 [2048, 768], P('ingest'), may hold values from -6 to 6
- assignment: int32 [98304], P(('index', 'ingest')), may hold values from 0 to 2047
- block_order: int32 [24, 32], P('index'), may hold values from 0 to 31, each once within a row
- destination: int32 [24, 32, 1], P('index'), may hold values from 0 to 23; in each aligned block of 32 rows (0 to 31, 32 to 63, ..., all dimensions but the last counted through in order) at most 3 rows name the same one
- live_count: int32 [24], P('index'), may hold values from 24 to 32
Outputs:
- rebalanced: bfloat16 [768, 221184], P('ingest', 'index')
The draws below stay inside these ranges and needn't reach their ends.
Inputs may be any that keep to these rules, and one draw needn't show every extreme that they name: In each owner's list of 32 entries no destination is named by more than 3 entries. `block_order`: each owner's list names each of its 32 blocks once.
All inputs are finite; a program needn't handle non-finite values.
Results may differ from the reference program's by a relative error of at most 0.01.
Values may be sent and summed in bfloat16 or wider, within the bound.
A program may use at most 32 MiB of HBM per device.

```python
import math
import jax
import jax.numpy as jnp
import numpy as np
from jax import lax

D = 768
BROWS = 128
LISTS = 2048
ROWS = 98304
GROUP_ROWS = 4096
BLK = 32
CAP = 3
N_INDEX = 24


def plant(result, rng, least, high):
    dims = result.shape
    index_at = [jax.random.randint(jax.random.fold_in(rng, axis), (), 0, dims[axis]) for axis in range(len(dims))]
    result = result.at[tuple(index_at)].set(least)
    longest = dims.index(max(dims))
    index_at[longest] = (index_at[longest] + 1) % dims[longest]
    return result.at[tuple(index_at)].set(high)


def steps_of(key, shape, pieces, smallest, top_value):
    loudness, own = 1.0, jax.random.fold_in(key, 6)
    for axis_at, shards_of in pieces:
        draws = jnp.exp(jax.random.uniform(jax.random.fold_in(own, axis_at), (shards_of,), jnp.float32, smallest / len(pieces), top_value / len(pieces)))
        loudness = loudness * jnp.repeat(draws, shape[axis_at] // shards_of).reshape([-1 if axis == axis_at else 1 for axis in range(len(shape))])
    return loudness


def rank_bounds(amount, skew):
    loads = [(1 << 20) // math.isqrt(rank ** skew) + 1 for rank in range(1, amount + 1)]
    spread = 1 + sum(loads) // (1 << 30)
    return np.cumsum(np.array([max(1, weight // spread) for weight in loads]))


def ranked_ids(key, extent, count, slope):
    listing = rank_bounds(count, slope)
    pick = jax.random.randint(jax.random.fold_in(key, 1), extent, 0, int(listing[count - 1]))
    grade = jnp.searchsorted(jnp.asarray(listing, jnp.int32), pick, side="right")
    return jax.random.permutation(jax.random.fold_in(key, 2), count)[grade].astype(jnp.int32)


def routed_block(own_key, own, number, rows, amount, top, bound, slope):
    order = jax.random.permutation(own_key, amount)
    packed, usual = portions_of(amount, rows * top, bound, slope, True), portions_of(amount, rows * top, bound, slope, False)
    places = jnp.arange(amount)

    def named(sizes, turn):
        used = int((sizes > 0).sum())
        fixed = max(1, used // 4)
        moved = fixed + (places - fixed + turn * (used - fixed)) % max(1, amount - fixed)
        return jnp.zeros((amount,), jnp.int32).at[order[jnp.where(places < fixed, places, moved)]].set(jnp.asarray(sizes, jnp.int32))

    sizes = jnp.where(number % 4 == 0, named(packed, number // 4), named(usual, number - number // 4 - 1))
    mixed = jax.random.permutation(jax.random.fold_in(own, 3), amount)
    donor, receiver = mixed[0:amount // 2 * 2:2], mixed[1:amount // 2 * 2:2]
    margin = jnp.minimum(sizes[donor] - 1, bound - sizes[receiver]) // 2
    margin = jnp.where((donor == order[0]) | (receiver == order[0]) | (sizes[receiver] == 0), 0, jnp.maximum(margin, 0))
    moved = jax.random.randint(jax.random.fold_in(own, 4), (amount // 2,), 0, 1 << 20) % (margin + 1)
    sizes = sizes.at[donor].add(-moved).at[receiver].add(moved)
    labels = jnp.searchsorted(jnp.cumsum(sizes), jnp.arange(rows * top), side="right").astype(jnp.int32)
    grid = labels.reshape(top, rows).T
    grid = grid[jax.random.permutation(jax.random.fold_in(own, 1), rows)]
    turn = jax.random.randint(jax.random.fold_in(own, 2), (rows, 1), 0, top)
    return jnp.take_along_axis(grid, (jnp.arange(top)[None, :] + turn) % top, axis=1)


def portions_of(amount, total, most, lean, full):
    weights = [(1 << 20) // math.isqrt(standing ** lean) + 1 for standing in range(1, amount + 1)]
    largest = most if full else min(most, max(-(-total // amount), total * weights[0] // sum(weights)))
    least = 1 if total - largest >= amount - 1 else 0
    counts, surplus = [largest] + [least] * (amount - 1), total - largest - least * (amount - 1)
    while surplus > 0:
        movable = [i for i in range(1, amount) if counts[i] < largest] or [i for i in range(1, amount) if counts[i] < most]
        whole, remaining = sum([weights[i] for i in movable]), surplus
        for i in movable:
            extra = min(most - counts[i], max(1, remaining * weights[i] // whole), surplus)
            counts[i] = counts[i] + extra
            surplus = surplus - extra
    return np.array(counts)


def centred(stream_key, extent, spread, most, pieces=(), held_as=jnp.bfloat16):
    array = jax.random.normal(stream_key, extent, jnp.float32) * spread
    if len(pieces) > 0:
        array = steps_of(stream_key, extent, pieces, -0.22, 0.18) * array
    return jnp.clip(array, min=-most, max=most).astype(held_as)


def setup_inputs(seed: int = 0) -> dict:
    key_of = jax.random.split(jax.random.key(seed), 8)
    vectors = centred(key_of[0], (ROWS, D), 1.0, 6.0, ((0, 768),))
    rotation = centred(key_of[1], (D, D), D ** -0.5, 0.21875)
    centroids = centred(key_of[2], (LISTS, D), 1.0, 6.0, ((0, 32),))
    assignment = plant(ranked_ids(key_of[3], (ROWS,), LISTS, 1), jax.random.fold_in(key_of[3], 3), 0, LISTS - 1).astype(jnp.int32)
    block_order = jax.vmap(lambda own: jax.random.permutation(own, BLK))(jax.random.split(key_of[4], N_INDEX)).reshape((N_INDEX, BLK)).astype(jnp.int32)
    destination_keys = jax.random.split(jax.random.fold_in(key_of[5], 1), N_INDEX * BLK // BLK)
    destination_turns = jax.random.permutation(jax.random.fold_in(key_of[5], 3), N_INDEX * BLK // BLK)
    destination = jax.vmap(lambda own, number: routed_block(jax.random.fold_in(key_of[5], 2), own, number, BLK, N_INDEX, 1, CAP, 2))(destination_keys, destination_turns).reshape((N_INDEX, BLK, 1))
    live_count = plant(jax.random.randint(key_of[6], (N_INDEX,), 3 * BLK // 4, BLK + 1), jax.random.fold_in(key_of[6], 1), 3 * BLK // 4, BLK).astype(jnp.int32)
    return dict(vectors=vectors, rotation=rotation, centroids=centroids, assignment=assignment, block_order=block_order, destination=destination, live_count=live_count)


def place_blocks(blocks, order, dest, count):
    entry = jnp.arange(BLK, dtype=jnp.int32)
    live = entry < count
    owners = jnp.arange(N_INDEX, dtype=jnp.int32)
    hits = ((dest[:, None] == owners[None, :]) & live[:, None]).astype(jnp.int32)
    before = jnp.cumsum(hits, axis=0) - hits
    slot = jnp.sum(before * hits, axis=1).astype(jnp.int32)
    target = jnp.where(live, dest * CAP + slot, N_INDEX * CAP).astype(jnp.int32)
    empty = jnp.zeros((N_INDEX * CAP, BROWS, D), jnp.bfloat16)
    return empty.at[target].set(blocks[order], mode="drop")


def reference(vectors, rotation, centroids, assignment, block_order, destination, live_count):
    turned = jnp.dot(centroids, rotation, preferred_element_type=jnp.float32).astype(jnp.bfloat16)

    def one_group(args):
        group, ids = args
        rotated = jnp.dot(group, rotation, preferred_element_type=jnp.float32).astype(jnp.bfloat16)
        looked = jnp.take(turned, ids, axis=0)
        return (rotated.astype(jnp.float32) - looked.astype(jnp.float32)).astype(jnp.bfloat16)

    residual = lax.map(one_group, (vectors.reshape(N_INDEX, GROUP_ROWS, D), assignment.reshape(N_INDEX, GROUP_ROWS)))
    blocks = residual.reshape(N_INDEX, BLK, BROWS, D)
    placed = jax.vmap(place_blocks)(blocks, block_order, destination[:, :, 0], live_count)
    placed = placed.reshape(N_INDEX, N_INDEX, CAP, BROWS, D)
    placed = jnp.transpose(placed, (4, 1, 0, 2, 3))
    return placed.reshape(D, N_INDEX * N_INDEX * CAP * BROWS)
```

```python
import jax
import jax.numpy as jnp
from jax import lax
from jax.experimental import pallas as pl
from jax.experimental.pallas import tpu as pltpu
from jax.sharding import PartitionSpec as P

D = 768
BROWS = 128
CAP = 3
NI = 24
NG = 32
FEAT = D // NG
HALF = 32
WIDE = CAP * BROWS
MESH = pl.DeviceIdType.MESH


def lanes(x, idx):
    return jnp.take_along_axis(x, idx, axis=1, mode="promise_in_bounds")


def kernel(vec, rot, cen, asg, order, dest, live, out,
           x, r, send, recv, tbl, grp, pos, looked, res, send2, blkv, blks,
           lsem, ssem, rsem, tsem, s2sem, r2sem):
    f32, bf16, i32 = jnp.float32, jnp.bfloat16, jnp.int32
    g = lax.axis_index("ingest")
    i = lax.axis_index("index")
    core = lax.rem(i, 2)
    zh = lax.rem(lax.div(i, 2), 3)
    xx = lax.div(i, 6)

    def peer(e):
        far = e < 16
        dz = jnp.where(far, 1 + lax.rem(e, 2), 0)
        rest = jnp.where(far, lax.div(e, 2), 23 - e)
        px = lax.rem(xx + lax.div(rest, 2), 4)
        pz = lax.rem(zh + dz, 3)
        pc = lax.rem(core + lax.rem(rest, 2), 2)
        return (px * 3 + pz) * 2 + pc

    barrier = pltpu.get_barrier_semaphore()

    @pl.loop(1, NG)
    def _(d):
        pl.semaphore_signal(barrier, inc=1, device_id={"ingest": lax.rem(g + d, NG)}, device_id_type=MESH)

    @pl.loop(0, NI - 1)
    def _(e):
        pl.semaphore_signal(barrier, inc=1, device_id={"index": peer(e)}, device_id_type=MESH)

    loads = [
        pltpu.make_async_copy(rot, r, lsem.at[0]),
        pltpu.make_async_copy(vec, x.at[pl.ds(0, BROWS)], lsem.at[1]),
    ]
    for k in range(4):
        loads.append(pltpu.make_async_copy(
            cen.at[pl.ds(pl.multiple_of(core * HALF, HALF), HALF)],
            x.at[pl.ds(BROWS + HALF * k, HALF)], lsem.at[2 + k]))
    for c in loads:
        c.start()

    sub = lax.broadcasted_iota(i32, (32, 32), 0)
    lan = lax.broadcasted_iota(i32, (32, 32), 1)
    eye = sub == lan
    d_row = jnp.broadcast_to(dest[...], (32, 32))
    d_col = jnp.sum(jnp.where(eye, d_row, 0), axis=1, keepdims=True)
    o_col = jnp.sum(jnp.where(eye, jnp.broadcast_to(order[...], (32, 32)), 0), axis=1, keepdims=True)
    n_live = live[0]
    slot = jnp.sum(jnp.where((d_row == d_col) & (lan < sub) & (lan < n_live), 1, 0), axis=1, keepdims=True)
    k_col = lax.broadcasted_iota(i32, (32, 1), 0)
    target = jnp.where(k_col < n_live, d_col * CAP + slot, -1)
    q = lax.broadcasted_iota(i32, (32, 128), 1)
    hit = target == q
    blk = jnp.sum(jnp.where(hit, o_col - NG, 0), axis=0, keepdims=True) + NG
    blkv[...] = jnp.broadcast_to(blk, (8, 128))
    to_smem = pltpu.make_async_copy(blkv, blks, lsem.at[6])
    to_smem.start()

    lane8 = lax.broadcasted_iota(i32, (8, 128), 1)
    sub8 = lax.broadcasted_iota(i32, (8, 128), 0)
    slot8 = lax.div(lane8, 32)
    low8 = lax.rem(lane8, 32)

    a = lanes(jnp.broadcast_to(asg[...], (8, 128)), lax.rem(sub8, 4) * 32 + low8)
    a_grp = (lax.shift_right_logical(a, 5) & 1) * 8 + lax.shift_right_logical(a, 8)
    a_pos = (lax.shift_right_logical(a, 6) & 3) * 32 + (a & 31)
    a_val = jnp.where(sub8 < 4, a_grp, a_pos).astype(f32)

    for c in loads:
        c.wait()
    y = jnp.dot(x[...], r[...], preferred_element_type=f32).astype(bf16).astype(f32)
    yt = y.T
    rt = yt[:, :BROWS].reshape(NG, FEAT, BROWS)
    tt = yt[:, BROWS:].reshape(NG, FEAT, BROWS)
    turn = lax.rem(slot8 + 4 - lax.rem(g, 4), 4)[None]
    tail = jnp.where(turn == 0, tt[:, 0:8], jnp.where(turn == 1, tt[:, 8:16], jnp.where(turn == 2, tt[:, 16:24], a_val[None])))
    send[...] = jnp.concatenate([rt, tail], axis=1).astype(bf16)

    pl.semaphore_wait(barrier, NG + NI - 2)

    @pl.loop(1, NG)
    def _(d):
        to = lax.rem(g + d, NG)
        pltpu.make_async_remote_copy(
            src_ref=send.at[to], dst_ref=recv.at[g], send_sem=ssem, recv_sem=rsem,
            device_id={"ingest": to}, device_id_type=MESH).start()

    recv[pl.ds(g, 1)] = send[pl.ds(g, 1)]
    res[NG] = jnp.zeros((FEAT, BROWS), bf16)
    to_smem.wait()

    some = pltpu.make_async_remote_copy(
        src_ref=send.at[pl.ds(0, NG - 1)], dst_ref=recv.at[pl.ds(0, NG - 1)], send_sem=ssem, recv_sem=rsem,
        device_id={"ingest": lax.rem(g + 1, NG)}, device_id_type=MESH)
    some.wait_recv()

    @pl.loop(0, NG // 4)
    def _(quad):
        m = [recv[quad * 4 + j].astype(f32)[24:32] for j in range(4)]
        turned = []
        for f in range(4):
            t = m[3]
            for j in range(3):
                t = jnp.where(slot8 == (f + j) % 4, m[j], t)
            turned.append(t)
        tbl[core, quad] = jnp.concatenate(turned[:3], axis=0).astype(bf16)
        for j in range(4):
            v = lanes(turned[3], 32 * ((3 + j) % 4) + low8)
            grp[pl.ds(quad * 4 + j, 1)] = jnp.sum(jnp.where(sub8 == slot8, v, 0.0), axis=0, keepdims=True).astype(i32)
            pos[pl.ds(quad * 4 + j, 1)] = jnp.sum(jnp.where(sub8 == slot8 + 4, v, 0.0), axis=0, keepdims=True).astype(i32)

    other = lax.rem(core + 1, 2)
    swap = pltpu.make_async_remote_copy(
        src_ref=tbl.at[core], dst_ref=tbl.at[core], send_sem=tsem.at[0], recv_sem=tsem.at[1],
        device_id={"index": i + 1 - 2 * core}, device_id_type=MESH)
    swap.start()

    def look(half, first):
        table = [tbl[half, quad].astype(f32) for quad in range(NG // 4)]

        @pl.loop(0, NG)
        def _(b):
            lane0 = jnp.broadcast_to(pos[pl.ds(b, 1)], (8, 128))
            want = jnp.broadcast_to(grp[pl.ds(b, 1)], (8, 128)) - half * (NG // 4)
            outs = []
            for f in range(3):
                idx = (lane0 + 32 * f) & 127
                acc = jnp.zeros((8, 128), f32) if first else looked[b, 8 * f:8 * f + 8]
                for quad in range(NG // 4):
                    acc = jnp.where(want == quad, lanes(table[quad][8 * f:8 * f + 8], idx), acc)
                outs.append(acc)
            got = jnp.concatenate(outs, axis=0)
            if first:
                looked[b] = got
            else:
                res[b] = (recv[b].astype(f32)[:FEAT] - got).astype(bf16)

    look(core, True)
    pltpu.make_async_remote_copy(
        src_ref=tbl.at[other], dst_ref=tbl.at[other], send_sem=tsem.at[0], recv_sem=tsem.at[1],
        device_id={"index": i + 1 - 2 * core}, device_id_type=MESH).wait_recv()
    look(other, False)

    def pack(p):
        for s in range(CAP):
            send2[p, :, s * BROWS:(s + 1) * BROWS] = res[blks[0, p * CAP + s]]

    columns = pl.ds(pl.multiple_of(i * WIDE, WIDE), WIDE)

    @pl.loop(0, NI - 1)
    def _(e):
        p = peer(e)
        pack(p)
        pltpu.make_async_remote_copy(
            src_ref=send2.at[p], dst_ref=out.at[:, columns], send_sem=s2sem.at[e], recv_sem=r2sem.at[e],
            device_id={"index": p}, device_id_type=MESH).start()

    pack(i)
    own = pltpu.make_async_copy(send2.at[i], out.at[:, columns], lsem.at[7])
    own.start()
    some.wait_send()
    swap.wait_send()
    own.wait()

    @pl.loop(0, NI - 1)
    def _(e):
        c = pltpu.make_async_remote_copy(
            src_ref=send2.at[0], dst_ref=out.at[:, pl.ds(0, WIDE)], send_sem=s2sem.at[e], recv_sem=r2sem.at[e],
            device_id={"index": peer(e)}, device_id_type=MESH)
        c.wait_send()
        c.wait_recv()


def body(vectors, rotation, centroids, assignment, block_order, destination, live_count):
    bf16, f32, i32 = jnp.bfloat16, jnp.float32, jnp.int32
    anywhere = pl.BlockSpec(memory_space=pl.ANY)
    vmem = pl.BlockSpec(memory_space=pltpu.VMEM)
    smem = pl.BlockSpec(memory_space=pltpu.SMEM)
    dma = pltpu.SemaphoreType.DMA
    return pl.pallas_call(
        kernel,
        out_shape=jax.ShapeDtypeStruct((FEAT, NI * WIDE), bf16),
        in_specs=[anywhere, anywhere, anywhere, vmem, vmem, vmem, smem],
        out_specs=anywhere,
        scratch_shapes=[
            pltpu.VMEM((2 * BROWS, D), bf16),
            pltpu.VMEM((D, D), bf16),
            pltpu.VMEM((NG, 32, BROWS), bf16),
            pltpu.VMEM((NG, 32, BROWS), bf16),
            pltpu.VMEM((2, NG // 4, FEAT, 128), bf16),
            pltpu.VMEM((NG, 128), i32),
            pltpu.VMEM((NG, 128), i32),
            pltpu.VMEM((NG, FEAT, 128), f32),
            pltpu.VMEM((NG + 1, FEAT, BROWS), bf16),
            pltpu.VMEM((NI, FEAT, WIDE), bf16),
            pltpu.VMEM((8, 128), i32),
            pltpu.SMEM((8, 128), i32),
            dma((8,)), dma, dma, dma((2,)), dma((NI,)), dma((NI,)),
        ],
        compiler_params=pltpu.CompilerParams(
            collective_id=0, has_side_effects=True, vmem_limit_bytes=32 * 1024 * 1024),
        name="route",
    )(vectors, rotation, centroids, assignment.reshape(1, BROWS), block_order, destination.reshape(1, 32), live_count)


def solution(mesh):
    return jax.shard_map(
        body,
        mesh=mesh,
        in_specs=(
            P(("index", "ingest"), None),
            P(),
            P("ingest", None),
            P(("index", "ingest")),
            P("index", None),
            P("index", None, None),
            P("index"),
        ),
        out_specs=P("ingest", "index"),
        check_vma=False,
    )
```

```python
import jax
import jax.numpy as jnp
from jax import lax
from jax.experimental import pallas as pl
from jax.experimental.pallas import tpu as pltpu
from jax.sharding import PartitionSpec as P

D = 768
BROWS = 128
CAP = 3
NI = 24
NG = 32
FEAT = D // NG
OCT = FEAT // 8
QUADS = NG // 4
FIRST = 2
HALF = 32
WIDE = CAP * BROWS
MESH = pl.DeviceIdType.MESH


def lanes(x, idx):
    return jnp.take_along_axis(x, idx, axis=1, mode="promise_in_bounds")


def kernel(vec, rot, cen, asg_in, order_in, dest_in, live, out,
           asg, order, dest, x, r, send, recv, sent_tail, tail_in, tbl, grp, pos, looked, send2, blkv, blks,
           lsem, s1, r1, swap_sem, s2, r2, entered, paired):
    f32, bf16, i32 = jnp.float32, jnp.bfloat16, jnp.int32
    g = lax.axis_index("ingest")
    i = lax.axis_index("index")
    core = i & 1
    chip = lax.shift_right_logical(i, 1)
    xx = lax.div(chip, 3)
    zh = chip - 3 * xx
    other = 1 - core
    spot = xx * 2 + core
    rank = zh * 8 + spot

    def ingest_peer(t):
        n = t >> 2
        dy = jnp.where((n & 1) == 0, 4 + (n >> 1), 3 - (n >> 1))
        return (((g >> 2) + dy) & 7) * 4 + ((g & 3) ^ (3 - (t & 3)))

    def owner(z, x_, c):
        return (x_ * 3 + z) * 2 + c

    sibling = owner(zh, xx, other)
    small = [
        pltpu.make_async_copy(a, b, lsem.at[8 + k])
        for k, (a, b) in enumerate(((asg_in, asg), (order_in, order), (dest_in, dest)))]
    for c in small:
        c.start()
    loads = [
        pltpu.make_async_copy(rot, r, lsem.at[0]),
        pltpu.make_async_copy(vec, x.at[pl.ds(0, BROWS)], lsem.at[1]),
    ]
    for k in range(4):
        loads.append(pltpu.make_async_copy(
            cen.at[pl.ds(pl.multiple_of(core * HALF, HALF), HALF)],
            x.at[pl.ds(BROWS + HALF * k, HALF)], lsem.at[2 + k]))
    for c in loads:
        c.start()

    barrier = pltpu.get_barrier_semaphore()

    @pl.loop(0, NG - 1, unroll=31)
    def _(t):
        pl.semaphore_signal(barrier, inc=1, device_id={"ingest": ingest_peer(t)}, device_id_type=MESH)

    @pl.loop(rank + 1, NI)
    def _(n):
        pl.semaphore_signal(
            barrier, inc=1, device_id={"index": owner(n >> 3, (n >> 1) & 3, n & 1)}, device_id_type=MESH)

    for c in small:
        c.wait()
    sub = lax.broadcasted_iota(i32, (32, 32), 0)
    lan = lax.broadcasted_iota(i32, (32, 32), 1)
    eye = sub == lan
    d_row = jnp.broadcast_to(dest[...], (32, 32))
    d_col = jnp.sum(jnp.where(eye, d_row, 0), axis=1, keepdims=True)
    o_col = jnp.sum(jnp.where(eye, jnp.broadcast_to(order[...], (32, 32)), 0), axis=1, keepdims=True)
    n_live = live[0]
    slot = jnp.sum(jnp.where((d_row == d_col) & (lan < sub) & (lan < n_live), 1, 0), axis=1, keepdims=True)
    k_col = lax.broadcasted_iota(i32, (32, 1), 0)
    target = jnp.where(k_col < n_live, d_col * CAP + slot, -1)
    q = lax.broadcasted_iota(i32, (32, 128), 1)
    blk = jnp.sum(jnp.where(target == q, o_col - NG, 0), axis=0, keepdims=True) + NG
    blkv[...] = jnp.broadcast_to(blk, (8, 128))
    to_smem = pltpu.make_async_copy(blkv, blks, lsem.at[6])
    to_smem.start()

    lane8 = lax.broadcasted_iota(i32, (8, 128), 1)
    sub8 = lax.broadcasted_iota(i32, (8, 128), 0)
    slot8 = lane8 >> 5
    low8 = lane8 & 31

    a = lanes(jnp.broadcast_to(asg[...], (8, 128)), (sub8 & 3) * 32 + low8)
    a_grp = ((a >> 5) & 1) * QUADS + (a >> 8)
    a_pos = ((a >> 6) & 3) * 32 + (a & 31)
    a_val = jnp.where(sub8 < 4, a_grp, a_pos).astype(f32)

    for c in loads:
        c.wait()
    y = jnp.dot(x[...], r[...], preferred_element_type=f32).astype(bf16).astype(f32)
    yt = y.T
    rt = yt[:, :BROWS].reshape(NG, OCT, 8, BROWS)
    tt = yt[:, BROWS:].reshape(NG, OCT, 8, BROWS)
    turn = ((slot8 - g) & 3)[None]
    tail = jnp.where(turn == 0, tt[:, 0], jnp.where(turn == 1, tt[:, 1], jnp.where(turn == 2, tt[:, 2], a_val[None])))
    sent_tail[...] = tail.astype(bf16)
    send[...] = rt.astype(bf16)

    pl.semaphore_wait(barrier, NG - 1 + rank)

    def scatter(k, src, dst):
        @pl.loop(0, NG - 1, unroll=31)
        def _(t):
            to = ingest_peer(t)
            pltpu.make_async_remote_copy(
                src_ref=src.at[to], dst_ref=dst.at[g], send_sem=s1.at[k], recv_sem=r1.at[k],
                device_id={"ingest": to}, device_id_type=MESH).start()

        return pltpu.make_async_remote_copy(
            src_ref=src.at[pl.ds(0, NG - 1)], dst_ref=dst.at[pl.ds(0, NG - 1)],
            send_sem=s1.at[k], recv_sem=r1.at[k],
            device_id={"ingest": (g + 1) & (NG - 1)}, device_id_type=MESH)

    tails = scatter(0, sent_tail, tail_in)
    features = scatter(1, send, recv)

    @pl.when(core == 1)
    def _():
        pl.semaphore_signal(paired, inc=1, device_id={"index": sibling}, device_id_type=MESH)

    @pl.loop(0, rank)
    def _(n):
        pl.semaphore_signal(
            entered.at[zh], inc=1, device_id={"index": owner(n >> 3, (n >> 1) & 3, n & 1)}, device_id_type=MESH)

    tail_in[pl.ds(g, 1)] = sent_tail[pl.ds(g, 1)]
    recv[pl.ds(g, 1)] = send[pl.ds(g, 1)]
    recv[NG] = jnp.zeros((OCT, 8, BROWS), bf16)
    looked[NG] = jnp.zeros((OCT, 8, BROWS), f32)
    to_smem.wait()

    tails.wait_recv()
    for quad in range(QUADS):
        m = [tail_in[quad * 4 + j].astype(f32) for j in range(4)]
        for f in range(4):
            t = m[3]
            for j in range(3):
                t = jnp.where(slot8 == (f + j) % 4, m[j], t)
            if f < OCT:
                tbl[core, quad, f] = t.astype(bf16)
        for j in range(4):
            v = lanes(t, 32 * ((3 + j) % 4) + low8)
            b = quad * 4 + j
            grp[b:b + 1] = jnp.sum(jnp.where(sub8 == slot8, v, 0.0), axis=0, keepdims=True).astype(i32)
            pos[b:b + 1] = jnp.sum(jnp.where(sub8 == slot8 + 4, v, 0.0), axis=0, keepdims=True).astype(i32)

    def swap(half):
        return pltpu.make_async_remote_copy(
            src_ref=tbl.at[half], dst_ref=tbl.at[half], send_sem=swap_sem.at[0], recv_sem=swap_sem.at[1],
            device_id={"index": sibling}, device_id_type=MESH)

    @pl.when(core == 0)
    def _():
        pl.semaphore_wait(paired, 1)

    swap(core).start()

    def look(half, first):
        table = [[tbl[half, quad, f].astype(f32) for f in range(OCT)] for quad in range(QUADS)]

        @pl.loop(0, NG, unroll=8)
        def _(b):
            lane0 = jnp.broadcast_to(pos[pl.ds(b, 1)], (8, 128))
            want = jnp.broadcast_to(grp[pl.ds(b, 1)], (8, 128)) - half * QUADS
            for f in range(OCT):
                idx = (lane0 + 32 * f) & 127
                acc = jnp.zeros((8, 128), f32) if first else looked[b, f]
                for quad in range(QUADS):
                    acc = jnp.where(want == quad, lanes(table[quad][f], idx), acc)
                looked[b, f] = acc

    look(core, True)
    swap(other).wait_recv()
    look(other, False)

    columns = pl.ds(pl.multiple_of(i * WIDE, WIDE), WIDE)

    def pack(p):
        for f in range(OCT):
            for s in range(CAP):
                b = blks[0, p * CAP + s]
                send2[p, f, :, s * BROWS:(s + 1) * BROWS] = (recv[b, f].astype(f32) - looked[b, f]).astype(bf16)

    def deliver(z, x_, c, sent):
        p = owner(z, x_, c)
        pack(p)
        pltpu.make_async_remote_copy(
            src_ref=send2.at[p], dst_ref=out.at[:, :, columns], send_sem=s2.at[sent], recv_sem=r2,
            device_id={"index": p}, device_id_type=MESH).start()

    features.wait_recv()

    def messages(n, sent):
        some = out.at[:, :, pl.ds(0, n * WIDE)]
        return pltpu.make_async_remote_copy(
            src_ref=some, dst_ref=some, send_sem=s2.at[sent], recv_sem=r2,
            device_id={"index": sibling}, device_id_type=MESH)

    def far(z, sent):
        @pl.when(z > zh)
        def _():
            pl.semaphore_wait(entered.at[z], 8)

        @pl.loop(0, 8)
        def _(m):
            deliver(z, (xx + ((m >> 1) ^ 2)) & 3, core ^ (m & 1), sent)

    step = 1 + jnp.where((g & 3) < FIRST, 1, 0)
    z0 = zh + step
    z0 = jnp.where(z0 >= 3, z0 - 3, z0)
    far(z0, 0)

    @pl.when(spot < 7)
    def _():
        pl.semaphore_wait(entered.at[zh], 7 - spot)

    @pl.loop(1, 8)
    def _(m):
        deliver(zh, (xx + (m >> 1)) & 3, core ^ (m & 1), 1)

    far(3 - zh - z0, 1)

    pack(i)
    own = pltpu.make_async_copy(send2.at[i], out.at[:, :, columns], lsem.at[7])
    own.start()
    tails.wait_send()
    features.wait_send()
    swap(core).wait_send()
    own.wait()

    messages(8, 0).wait_send()
    messages(NI - 9, 1).wait_send()
    messages(NI - 1, 1).wait_recv()


def body(vectors, rotation, centroids, assignment, block_order, destination, live_count):
    bf16, f32, i32 = jnp.bfloat16, jnp.float32, jnp.int32
    hbm = pl.BlockSpec(memory_space=pltpu.HBM)
    smem = pl.BlockSpec(memory_space=pltpu.SMEM)
    dma = pltpu.SemaphoreType.DMA
    arrays = [
        pltpu.with_memory_space_constraint(a, pltpu.HBM)
        for a in (vectors, rotation, centroids, assignment.reshape(1, BROWS), block_order, destination.reshape(1, NG))]
    rebalanced = pl.pallas_call(
        kernel,
        out_shape=jax.ShapeDtypeStruct((OCT, 8, NI * WIDE), bf16),
        in_specs=[hbm] * 6 + [smem],
        out_specs=pl.BlockSpec(memory_space=pl.ANY),
        scratch_shapes=[
            pltpu.VMEM((1, BROWS), i32),
            pltpu.VMEM((1, NG), i32),
            pltpu.VMEM((1, NG), i32),
            pltpu.VMEM((2 * BROWS, D), bf16),
            pltpu.VMEM((D, D), bf16),
            pltpu.VMEM((NG, OCT, 8, BROWS), bf16),
            pltpu.VMEM((NG + 1, OCT, 8, BROWS), bf16),
            pltpu.VMEM((NG, 8, BROWS), bf16),
            pltpu.VMEM((NG, 8, BROWS), bf16),
            pltpu.VMEM((2, QUADS, OCT, 8, 128), bf16),
            pltpu.VMEM((NG, 128), i32),
            pltpu.VMEM((NG, 128), i32),
            pltpu.VMEM((NG + 1, OCT, 8, 128), f32),
            pltpu.VMEM((NI, OCT, 8, WIDE), bf16),
            pltpu.VMEM((8, 128), i32),
            pltpu.SMEM((8, 128), i32),
            dma((11,)), dma((2,)), dma((2,)), dma((2,)), dma((2,)), dma,
            pltpu.SemaphoreType.REGULAR((3,)), pltpu.SemaphoreType.REGULAR,
        ],
        compiler_params=pltpu.CompilerParams(
            collective_id=0, has_side_effects=True, vmem_limit_bytes=40 * 1024 * 1024),
        name="route",
    )(*arrays, live_count)
    return rebalanced.reshape(FEAT, NI * WIDE)


def solution(mesh):
    return jax.shard_map(
        body,
        mesh=mesh,
        in_specs=(
            P(("index", "ingest"), None),
            P(),
            P("ingest", None),
            P(("index", "ingest")),
            P("index", None),
            P("index", None, None),
            P("index"),
        ),
        out_specs=P("ingest", "index"),
        check_vma=False,
    )
```

```python
import jax
import jax.numpy as jnp
from jax import lax
from jax.experimental import pallas as pl
from jax.experimental.pallas import tpu as pltpu
from jax.sharding import PartitionSpec as P

D = 768
BROWS = 128
CAP = 3
NI = 24
NG = 32
FEAT = D // NG
OCT = FEAT // 8
QUADS = NG // 4
FIRST = 2
AHEAD = 1
HALF = 32
WIDE = CAP * BROWS
MESH = pl.DeviceIdType.MESH


def lanes(x, idx):
    return jnp.take_along_axis(x, idx, axis=1, mode="promise_in_bounds")


def kernel(vec, rot, cen, asg_in, order_in, dest_in, live, out,
           asg, order, dest, x, r, send, recv, sent_tail, tail_in, tbl, grp, pos, looked, send2, blkv, blks,
           lsem, s1, r1, swap_sem, s2, r2, entered, paired):
    f32, bf16, i32 = jnp.float32, jnp.bfloat16, jnp.int32
    g = lax.axis_index("ingest")
    i = lax.axis_index("index")
    core = i & 1
    chip = lax.shift_right_logical(i, 1)
    xx = lax.div(chip, 3)
    zh = chip - 3 * xx
    other = 1 - core
    spot = xx * 2 + core
    rank = zh * 8 + spot

    def ingest_peer(t):
        n = t >> 2
        dy = jnp.where((n & 1) == 0, 4 + (n >> 1), 3 - (n >> 1))
        return (((g >> 2) + dy) & 7) * 4 + ((g & 3) ^ (3 - (t & 3)))

    def owner(z, x_, c):
        return (x_ * 3 + z) * 2 + c

    sibling = owner(zh, xx, other)
    barrier = pltpu.get_barrier_semaphore()

    @pl.loop(0, NG - 1, unroll=31)
    def _(t):
        pl.semaphore_signal(barrier, inc=1, device_id={"ingest": ingest_peer(t)}, device_id_type=MESH)

    small = [
        pltpu.make_async_copy(a, b, lsem.at[8 + k])
        for k, (a, b) in enumerate(((asg_in, asg), (order_in, order), (dest_in, dest)))]
    for c in small:
        c.start()
    loads = [
        pltpu.make_async_copy(rot, r, lsem.at[0]),
        pltpu.make_async_copy(vec, x.at[pl.ds(0, BROWS)], lsem.at[1]),
    ]
    for k in range(4):
        loads.append(pltpu.make_async_copy(
            cen.at[pl.ds(pl.multiple_of(core * HALF, HALF), HALF)],
            x.at[pl.ds(BROWS + HALF * k, HALF)], lsem.at[2 + k]))
    for c in loads:
        c.start()

    @pl.loop(rank + 1, NI)
    def _(n):
        pl.semaphore_signal(
            barrier, inc=1, device_id={"index": owner(n >> 3, (n >> 1) & 3, n & 1)}, device_id_type=MESH)

    for c in small:
        c.wait()
    sub = lax.broadcasted_iota(i32, (32, 32), 0)
    lan = lax.broadcasted_iota(i32, (32, 32), 1)
    eye = sub == lan
    d_row = jnp.broadcast_to(dest[...], (32, 32))
    d_col = jnp.sum(jnp.where(eye, d_row, 0), axis=1, keepdims=True)
    o_col = jnp.sum(jnp.where(eye, jnp.broadcast_to(order[...], (32, 32)), 0), axis=1, keepdims=True)
    n_live = live[0]
    slot = jnp.sum(jnp.where((d_row == d_col) & (lan < sub) & (lan < n_live), 1, 0), axis=1, keepdims=True)
    k_col = lax.broadcasted_iota(i32, (32, 1), 0)
    target = jnp.where(k_col < n_live, d_col * CAP + slot, -1)
    q = lax.broadcasted_iota(i32, (32, 128), 1)
    blk = jnp.sum(jnp.where(target == q, o_col - NG, 0), axis=0, keepdims=True) + NG
    blkv[...] = jnp.broadcast_to(blk, (8, 128))
    to_smem = pltpu.make_async_copy(blkv, blks, lsem.at[6])
    to_smem.start()

    lane8 = lax.broadcasted_iota(i32, (8, 128), 1)
    sub8 = lax.broadcasted_iota(i32, (8, 128), 0)
    slot8 = lane8 >> 5
    low8 = lane8 & 31

    a = lanes(jnp.broadcast_to(asg[...], (8, 128)), (sub8 & 3) * 32 + low8)
    a_grp = ((a >> 5) & 1) * QUADS + (a >> 8)
    a_pos = ((a >> 6) & 3) * 32 + (a & 31)
    a_val = jnp.where(sub8 < 4, a_grp, a_pos).astype(f32)

    for c in loads:
        c.wait()
    y = jnp.dot(x[...], r[...], preferred_element_type=f32).astype(bf16).astype(f32)
    yt = y.T
    rt = yt[:, :BROWS].reshape(NG, OCT, 8, BROWS)
    tt = yt[:, BROWS:].reshape(NG, OCT, 8, BROWS)
    turn = ((slot8 - g) & 3)[None]
    tail = jnp.where(turn == 0, tt[:, 0], jnp.where(turn == 1, tt[:, 1], jnp.where(turn == 2, tt[:, 2], a_val[None])))
    sent_tail[...] = tail.astype(bf16)
    send[...] = rt.astype(bf16)

    pl.semaphore_wait(barrier, NG - 1 + rank)

    def scatter(k, src, dst):
        @pl.loop(0, NG - 1, unroll=31)
        def _(t):
            to = ingest_peer(t)
            pltpu.make_async_remote_copy(
                src_ref=src.at[to], dst_ref=dst.at[g], send_sem=s1.at[k], recv_sem=r1.at[k],
                device_id={"ingest": to}, device_id_type=MESH).start()

        return pltpu.make_async_remote_copy(
            src_ref=src.at[pl.ds(0, NG - 1)], dst_ref=dst.at[pl.ds(0, NG - 1)],
            send_sem=s1.at[k], recv_sem=r1.at[k],
            device_id={"ingest": (g + 1) & (NG - 1)}, device_id_type=MESH)

    @pl.when(core == 1)
    def _():
        pl.semaphore_signal(paired, inc=1, device_id={"index": sibling}, device_id_type=MESH)

    @pl.loop(0, rank)
    def _(n):
        pl.semaphore_signal(
            entered.at[zh], inc=1, device_id={"index": owner(n >> 3, (n >> 1) & 3, n & 1)}, device_id_type=MESH)

    tails = scatter(0, sent_tail, tail_in)
    features = scatter(1, send, recv)


    tail_in[pl.ds(g, 1)] = sent_tail[pl.ds(g, 1)]
    recv[pl.ds(g, 1)] = send[pl.ds(g, 1)]
    recv[NG] = jnp.zeros((OCT, 8, BROWS), bf16)
    looked[NG] = jnp.zeros((OCT, 8, BROWS), f32)
    to_smem.wait()

    tails.wait_recv()
    slips = []
    for quad in range(QUADS):
        m = [tail_in[quad * 4 + j].astype(f32) for j in range(4)]
        for f in range(4):
            t = m[3]
            for j in range(3):
                t = jnp.where(slot8 == (f + j) % 4, m[j], t)
            if f < OCT:
                tbl[core, quad, f] = t.astype(bf16)
        slips.append(t)

    def swap(half):
        return pltpu.make_async_remote_copy(
            src_ref=tbl.at[half], dst_ref=tbl.at[half], send_sem=swap_sem.at[0], recv_sem=swap_sem.at[1],
            device_id={"index": sibling}, device_id_type=MESH)

    @pl.when(core == 0)
    def _():
        pl.semaphore_wait(paired, 1)

    swap(core).start()

    for b in range(NG):
        v = lanes(slips[b // 4], 32 * ((3 + b) % 4) + low8)
        grp[b:b + 1] = jnp.sum(jnp.where(sub8 == slot8, v, 0.0), axis=0, keepdims=True).astype(i32)
        pos[b:b + 1] = jnp.sum(jnp.where(sub8 == slot8 + 4, v, 0.0), axis=0, keepdims=True).astype(i32)

    def look(half, first):
        table = [[tbl[half, quad, f].astype(f32) for f in range(OCT)] for quad in range(QUADS)]

        @pl.loop(0, NG, unroll=16)
        def _(b):
            lane0 = jnp.broadcast_to(pos[pl.ds(b, 1)], (8, 128))
            want = jnp.broadcast_to(grp[pl.ds(b, 1)], (8, 128)) - half * QUADS
            for f in range(OCT):
                idx = (lane0 + 32 * f) & 127
                acc = jnp.zeros((8, 128), f32) if first else looked[b, f]
                for quad in range(QUADS):
                    acc = jnp.where(want == quad, lanes(table[quad][f], idx), acc)
                looked[b, f] = acc

    look(core, True)
    swap(other).wait_recv()
    look(other, False)

    columns = pl.ds(pl.multiple_of(i * WIDE, WIDE), WIDE)

    def pack(p):
        for f in range(OCT):
            for s in range(CAP):
                b = blks[0, p * CAP + s]
                send2[p, f, :, s * BROWS:(s + 1) * BROWS] = (recv[b, f].astype(f32) - looked[b, f]).astype(bf16)

    def deliver(z, x_, c, sent):
        p = owner(z, x_, c)
        pack(p)
        pltpu.make_async_remote_copy(
            src_ref=send2.at[p], dst_ref=out.at[:, :, columns], send_sem=s2.at[sent], recv_sem=r2,
            device_id={"index": p}, device_id_type=MESH).start()

    features.wait_recv()

    def messages(n, sent):
        some = out.at[:, :, pl.ds(0, n * WIDE)]
        return pltpu.make_async_remote_copy(
            src_ref=some, dst_ref=some, send_sem=s2.at[sent], recv_sem=r2,
            device_id={"index": sibling}, device_id_type=MESH)

    def far(z, ahead):
        @pl.when(z > zh)
        def _():
            pl.semaphore_wait(entered.at[z], 8)

        @pl.loop(0, 8)
        def _(m):
            k = m >> 1
            x_ = (xx + jnp.where(k < 2, k + 2, 3 - k)) & 3
            deliver(z, x_, core ^ (m & 1), jnp.where(m < ahead, 0, 1))

    step = 1 + jnp.where((g & 3) < FIRST, 1, 0)
    z0 = zh + step
    z0 = jnp.where(z0 >= 3, z0 - 3, z0)
    far(z0, AHEAD)

    @pl.when(spot < 7)
    def _():
        pl.semaphore_wait(entered.at[zh], 7 - spot)

    @pl.loop(1, 8)
    def _(m):
        deliver(zh, (xx + (m >> 1)) & 3, core ^ (m & 1), 1)

    far(3 - zh - z0, 0)

    pack(i)
    own = pltpu.make_async_copy(send2.at[i], out.at[:, :, columns], lsem.at[7])
    own.start()
    tails.wait_send()
    features.wait_send()
    swap(core).wait_send()
    own.wait()

    messages(AHEAD, 0).wait_send()
    messages(NI - 1 - AHEAD, 1).wait_send()
    messages(NI - 1, 1).wait_recv()


def body(vectors, rotation, centroids, assignment, block_order, destination, live_count):
    bf16, f32, i32 = jnp.bfloat16, jnp.float32, jnp.int32
    hbm = pl.BlockSpec(memory_space=pltpu.HBM)
    smem = pl.BlockSpec(memory_space=pltpu.SMEM)
    dma = pltpu.SemaphoreType.DMA
    arrays = [
        pltpu.with_memory_space_constraint(a, pltpu.HBM)
        for a in (vectors, rotation, centroids, assignment.reshape(1, BROWS), block_order, destination.reshape(1, NG))]
    rebalanced = pl.pallas_call(
        kernel,
        out_shape=jax.ShapeDtypeStruct((OCT, 8, NI * WIDE), bf16),
        in_specs=[hbm] * 6 + [smem],
        out_specs=pl.BlockSpec(memory_space=pl.ANY),
        scratch_shapes=[
            pltpu.VMEM((1, BROWS), i32),
            pltpu.VMEM((1, NG), i32),
            pltpu.VMEM((1, NG), i32),
            pltpu.VMEM((2 * BROWS, D), bf16),
            pltpu.VMEM((D, D), bf16),
            pltpu.VMEM((NG, OCT, 8, BROWS), bf16),
            pltpu.VMEM((NG + 1, OCT, 8, BROWS), bf16),
            pltpu.VMEM((NG, 8, BROWS), bf16),
            pltpu.VMEM((NG, 8, BROWS), bf16),
            pltpu.VMEM((2, QUADS, OCT, 8, 128), bf16),
            pltpu.VMEM((NG, 128), i32),
            pltpu.VMEM((NG, 128), i32),
            pltpu.VMEM((NG + 1, OCT, 8, 128), f32),
            pltpu.VMEM((NI, OCT, 8, WIDE), bf16),
            pltpu.VMEM((8, 128), i32),
            pltpu.SMEM((8, 128), i32),
            dma((11,)), dma((2,)), dma((2,)), dma((2,)), dma((2,)), dma,
            pltpu.SemaphoreType.REGULAR((3,)), pltpu.SemaphoreType.REGULAR,
        ],
        compiler_params=pltpu.CompilerParams(
            collective_id=0, has_side_effects=True, vmem_limit_bytes=40 * 1024 * 1024),
        name="route",
    )(*arrays, live_count)
    return rebalanced.reshape(FEAT, NI * WIDE)


def solution(mesh):
    return jax.shard_map(
        body,
        mesh=mesh,
        in_specs=(
            P(("index", "ingest"), None),
            P(),
            P("ingest", None),
            P(("index", "ingest")),
            P("index", None),
            P("index", None, None),
            P("index"),
        ),
        out_specs=P("ingest", "index"),
        check_vma=False,
    )
```

```python
import jax
import jax.numpy as jnp
from jax import lax
from jax.experimental import pallas as pl
from jax.experimental.pallas import tpu as pltpu
from jax.sharding import PartitionSpec as P

D = 768
BROWS = 128
CAP = 3
NI = 24
NG = 32
FEAT = D // NG
OCT = FEAT // 8
QUADS = NG // 4
FIRST = 2
AHEAD = 1
HALF = 32
WIDE = CAP * BROWS
MESH = pl.DeviceIdType.MESH


def lanes(x, idx):
    return jnp.take_along_axis(x, idx, axis=1, mode="promise_in_bounds")


def kernel(vec, rot, cen, asg_in, order_in, dest_in, live, out,
           asg, order, dest, x, r, send, recv, sent_tail, tail_in, tbl, grp, pos, looked, send2, blkv, blks,
           lsem, s1, r1, swap_sem, s2, r2, entered, paired):
    f32, bf16, i32 = jnp.float32, jnp.bfloat16, jnp.int32
    g = lax.axis_index("ingest")
    i = lax.axis_index("index")
    core = i & 1
    chip = lax.shift_right_logical(i, 1)
    xx = lax.div(chip, 3)
    zh = chip - 3 * xx
    other = 1 - core
    spot = xx * 2 + core
    rank = zh * 8 + spot

    def ingest_peer(t):
        n = t & 7
        dy = jnp.where((n & 1) == 0, 4 - (n >> 1), 5 + (n >> 1)) & 7
        return (((g >> 2) + dy) & 7) * 4 + ((g & 3) ^ (3 - (t >> 3)))

    def owner(z, x_, c):
        return (x_ * 3 + z) * 2 + c

    sibling = owner(zh, xx, other)
    barrier = pltpu.get_barrier_semaphore()

    @pl.loop(0, NG - 1, unroll=31)
    def _(t):
        pl.semaphore_signal(barrier, inc=1, device_id={"ingest": ingest_peer(t)}, device_id_type=MESH)

    small = [
        pltpu.make_async_copy(a, b, lsem.at[8 + k])
        for k, (a, b) in enumerate(((asg_in, asg), (order_in, order), (dest_in, dest)))]
    for c in small:
        c.start()
    loads = [
        pltpu.make_async_copy(rot, r, lsem.at[0]),
        pltpu.make_async_copy(vec, x.at[pl.ds(0, BROWS)], lsem.at[1]),
    ]
    for k in range(4):
        loads.append(pltpu.make_async_copy(
            cen.at[pl.ds(pl.multiple_of(core * HALF, HALF), HALF)],
            x.at[pl.ds(BROWS + HALF * k, HALF)], lsem.at[2 + k]))
    for c in loads:
        c.start()

    @pl.loop(rank + 1, NI)
    def _(n):
        pl.semaphore_signal(
            barrier, inc=1, device_id={"index": owner(n >> 3, (n >> 1) & 3, n & 1)}, device_id_type=MESH)

    for c in small:
        c.wait()
    sub = lax.broadcasted_iota(i32, (32, 32), 0)
    lan = lax.broadcasted_iota(i32, (32, 32), 1)
    eye = sub == lan
    d_row = jnp.broadcast_to(dest[...], (32, 32))
    d_col = jnp.sum(jnp.where(eye, d_row, 0), axis=1, keepdims=True)
    o_col = jnp.sum(jnp.where(eye, jnp.broadcast_to(order[...], (32, 32)), 0), axis=1, keepdims=True)
    n_live = live[0]
    slot = jnp.sum(jnp.where((d_row == d_col) & (lan < sub) & (lan < n_live), 1, 0), axis=1, keepdims=True)
    k_col = lax.broadcasted_iota(i32, (32, 1), 0)
    target = jnp.where(k_col < n_live, d_col * CAP + slot, -1)
    q = lax.broadcasted_iota(i32, (32, 128), 1)
    blk = jnp.sum(jnp.where(target == q, o_col - NG, 0), axis=0, keepdims=True) + NG
    blkv[...] = jnp.broadcast_to(blk, (8, 128))
    to_smem = pltpu.make_async_copy(blkv, blks, lsem.at[6])
    to_smem.start()

    lane8 = lax.broadcasted_iota(i32, (8, 128), 1)
    sub8 = lax.broadcasted_iota(i32, (8, 128), 0)
    slot8 = lane8 >> 5
    low8 = lane8 & 31

    a = lanes(jnp.broadcast_to(asg[...], (8, 128)), (sub8 & 3) * 32 + low8)
    a_grp = ((a >> 5) & 1) * QUADS + (a >> 8)
    a_pos = ((a >> 6) & 3) * 32 + (a & 31)
    a_val = jnp.where(sub8 < 4, a_grp, a_pos).astype(f32)

    for c in loads:
        c.wait()
    y = jnp.dot(x[...], r[...], preferred_element_type=f32).astype(bf16).astype(f32)
    yt = y.T
    rt = yt[:, :BROWS].reshape(NG, OCT, 8, BROWS)
    tt = yt[:, BROWS:].reshape(NG, OCT, 8, BROWS)
    turn = ((slot8 - g) & 3)[None]
    tail = jnp.where(turn == 0, tt[:, 0], jnp.where(turn == 1, tt[:, 1], jnp.where(turn == 2, tt[:, 2], a_val[None])))
    sent_tail[...] = tail.astype(bf16)
    send[...] = rt.astype(bf16)

    pl.semaphore_wait(barrier, NG - 1 + rank)

    def scatter(k, src, dst):
        @pl.loop(0, NG - 1, unroll=31)
        def _(t):
            to = ingest_peer(t)
            pltpu.make_async_remote_copy(
                src_ref=src.at[to], dst_ref=dst.at[g], send_sem=s1.at[k], recv_sem=r1.at[k],
                device_id={"ingest": to}, device_id_type=MESH).start()

        return pltpu.make_async_remote_copy(
            src_ref=src.at[pl.ds(0, NG - 1)], dst_ref=dst.at[pl.ds(0, NG - 1)],
            send_sem=s1.at[k], recv_sem=r1.at[k],
            device_id={"ingest": (g + 1) & (NG - 1)}, device_id_type=MESH)

    @pl.when(core == 1)
    def _():
        pl.semaphore_signal(paired, inc=1, device_id={"index": sibling}, device_id_type=MESH)

    @pl.loop(0, rank)
    def _(n):
        pl.semaphore_signal(
            entered.at[zh], inc=1, device_id={"index": owner(n >> 3, (n >> 1) & 3, n & 1)}, device_id_type=MESH)

    tails = scatter(0, sent_tail, tail_in)
    features = scatter(1, send, recv)


    tail_in[pl.ds(g, 1)] = sent_tail[pl.ds(g, 1)]
    recv[pl.ds(g, 1)] = send[pl.ds(g, 1)]
    recv[NG] = jnp.zeros((OCT, 8, BROWS), bf16)
    looked[NG] = jnp.zeros((OCT, 8, BROWS), f32)
    to_smem.wait()

    tails.wait_recv()
    slips = []
    for quad in range(QUADS):
        m = [tail_in[quad * 4 + j].astype(f32) for j in range(4)]
        for f in range(4):
            t = m[3]
            for j in range(3):
                t = jnp.where(slot8 == (f + j) % 4, m[j], t)
            if f < OCT:
                tbl[core, quad, f] = t.astype(bf16)
        slips.append(t)

    def swap(half):
        return pltpu.make_async_remote_copy(
            src_ref=tbl.at[half], dst_ref=tbl.at[half], send_sem=swap_sem.at[0], recv_sem=swap_sem.at[1],
            device_id={"index": sibling}, device_id_type=MESH)

    @pl.when(core == 0)
    def _():
        pl.semaphore_wait(paired, 1)

    swap(core).start()

    for b in range(NG):
        v = lanes(slips[b // 4], 32 * ((3 + b) % 4) + low8)
        grp[b:b + 1] = jnp.sum(jnp.where(sub8 == slot8, v, 0.0), axis=0, keepdims=True).astype(i32)
        pos[b:b + 1] = jnp.sum(jnp.where(sub8 == slot8 + 4, v, 0.0), axis=0, keepdims=True).astype(i32)

    def look(half, first):
        table = [[tbl[half, quad, f].astype(f32) for f in range(OCT)] for quad in range(QUADS)]

        @pl.loop(0, NG, unroll=16)
        def _(b):
            lane0 = jnp.broadcast_to(pos[pl.ds(b, 1)], (8, 128))
            want = jnp.broadcast_to(grp[pl.ds(b, 1)], (8, 128)) - half * QUADS
            for f in range(OCT):
                idx = (lane0 + 32 * f) & 127
                acc = jnp.zeros((8, 128), f32) if first else looked[b, f]
                for quad in range(QUADS):
                    acc = jnp.where(want == quad, lanes(table[quad][f], idx), acc)
                looked[b, f] = acc

    look(core, True)
    swap(other).wait_recv()
    look(other, False)

    columns = pl.ds(pl.multiple_of(i * WIDE, WIDE), WIDE)

    def pack(p):
        for f in range(OCT):
            for s in range(CAP):
                b = blks[0, p * CAP + s]
                send2[p, f, :, s * BROWS:(s + 1) * BROWS] = (recv[b, f].astype(f32) - looked[b, f]).astype(bf16)

    def deliver(z, x_, c, sent):
        p = owner(z, x_, c)
        pack(p)
        pltpu.make_async_remote_copy(
            src_ref=send2.at[p], dst_ref=out.at[:, :, columns], send_sem=s2.at[sent], recv_sem=r2,
            device_id={"index": p}, device_id_type=MESH).start()

    features.wait_recv()

    def messages(n, sent):
        some = out.at[:, :, pl.ds(0, n * WIDE)]
        return pltpu.make_async_remote_copy(
            src_ref=some, dst_ref=some, send_sem=s2.at[sent], recv_sem=r2,
            device_id={"index": sibling}, device_id_type=MESH)

    def far(z, ahead):
        @pl.when(z > zh)
        def _():
            pl.semaphore_wait(entered.at[z], 8)

        @pl.loop(0, 8)
        def _(m):
            k = m >> 1
            x_ = (xx + jnp.where(k == 3, 0, jnp.where(k == 0, 2, 2 * k - 1))) & 3
            deliver(z, x_, core ^ (m & 1), jnp.where(m < ahead, 0, 1))

    step = 1 + jnp.where((zh == 1) | ((zh == 0) & ((g & 3) < FIRST)), 1, 0)
    z0 = zh + step
    z0 = jnp.where(z0 >= 3, z0 - 3, z0)
    far(z0, AHEAD)

    @pl.when(spot < 7)
    def _():
        pl.semaphore_wait(entered.at[zh], 7 - spot)

    @pl.loop(1, 8)
    def _(m):
        deliver(zh, (xx + (m >> 1)) & 3, core ^ (m & 1), 1)

    far(3 - zh - z0, 0)

    pack(i)
    own = pltpu.make_async_copy(send2.at[i], out.at[:, :, columns], lsem.at[7])
    own.start()
    tails.wait_send()
    features.wait_send()
    swap(core).wait_send()
    own.wait()

    messages(AHEAD, 0).wait_send()
    messages(NI - 1 - AHEAD, 1).wait_send()
    messages(NI - 1, 1).wait_recv()


def body(vectors, rotation, centroids, assignment, block_order, destination, live_count):
    bf16, f32, i32 = jnp.bfloat16, jnp.float32, jnp.int32
    hbm = pl.BlockSpec(memory_space=pltpu.HBM)
    smem = pl.BlockSpec(memory_space=pltpu.SMEM)
    dma = pltpu.SemaphoreType.DMA
    arrays = [
        pltpu.with_memory_space_constraint(a, pltpu.HBM)
        for a in (vectors, rotation, centroids, assignment.reshape(1, BROWS), block_order, destination.reshape(1, NG))]
    rebalanced = pl.pallas_call(
        kernel,
        out_shape=jax.ShapeDtypeStruct((OCT, 8, NI * WIDE), bf16),
        in_specs=[hbm] * 6 + [smem],
        out_specs=pl.BlockSpec(memory_space=pl.ANY),
        scratch_shapes=[
            pltpu.VMEM((1, BROWS), i32),
            pltpu.VMEM((1, NG), i32),
            pltpu.VMEM((1, NG), i32),
            pltpu.VMEM((2 * BROWS, D), bf16),
            pltpu.VMEM((D, D), bf16),
            pltpu.VMEM((NG, OCT, 8, BROWS), bf16),
            pltpu.VMEM((NG + 1, OCT, 8, BROWS), bf16),
            pltpu.VMEM((NG, 8, BROWS), bf16),
            pltpu.VMEM((NG, 8, BROWS), bf16),
            pltpu.VMEM((2, QUADS, OCT, 8, 128), bf16),
            pltpu.VMEM((NG, 128), i32),
            pltpu.VMEM((NG, 128), i32),
            pltpu.VMEM((NG + 1, OCT, 8, 128), f32),
            pltpu.VMEM((NI, OCT, 8, WIDE), bf16),
            pltpu.VMEM((8, 128), i32),
            pltpu.SMEM((8, 128), i32),
            dma((11,)), dma((2,)), dma((2,)), dma((2,)), dma((2,)), dma,
            pltpu.SemaphoreType.REGULAR((3,)), pltpu.SemaphoreType.REGULAR,
        ],
        compiler_params=pltpu.CompilerParams(
            collective_id=0, has_side_effects=True, vmem_limit_bytes=40 * 1024 * 1024),
        name="route",
    )(*arrays, live_count)
    return rebalanced.reshape(FEAT, NI * WIDE)


def solution(mesh):
    return jax.shard_map(
        body,
        mesh=mesh,
        in_specs=(
            P(("index", "ingest"), None),
            P(),
            P("ingest", None),
            P(("index", "ingest")),
            P("index", None),
            P("index", None, None),
            P("index"),
        ),
        out_specs=P("ingest", "index"),
        check_vma=False,
    )
```

```python
import jax
import jax.numpy as jnp
from jax import lax
from jax.experimental import pallas as pl
from jax.experimental.pallas import tpu as pltpu
from jax.sharding import PartitionSpec as P

D = 768
BROWS = 128
CAP = 3
NI = 24
NG = 32
FEAT = D // NG
OCT = FEAT // 8
QUADS = NG // 4
FIRST = 2
AHEAD = 1
HALF = 32
WIDE = CAP * BROWS
MESH = pl.DeviceIdType.MESH


def lanes(x, idx):
    return jnp.take_along_axis(x, idx, axis=1, mode="promise_in_bounds")


def kernel(vec, rot, cen, asg_in, order_in, dest_in, live, out,
           asg, order, dest, x, r, send, recv, sent_tail, tail_in, tbl, grp, pos, looked, send2, blkv, blks,
           lsem, s1, r1, swap_sem, s2, r2, entered, paired):
    f32, bf16, i32 = jnp.float32, jnp.bfloat16, jnp.int32
    g = lax.axis_index("ingest")
    i = lax.axis_index("index")
    core = i & 1
    chip = lax.shift_right_logical(i, 1)
    xx = lax.div(chip, 3)
    zh = chip - 3 * xx
    other = 1 - core
    spot = xx * 2 + core
    rank = zh * 8 + spot

    def ingest_peer(t):
        n = t & 7
        dy = jnp.where((n & 1) == 0, 4 - (n >> 1), 5 + (n >> 1)) & 7
        return (((g >> 2) + dy) & 7) * 4 + ((g & 3) ^ (3 - (t >> 3)))

    def owner(z, x_, c):
        return (x_ * 3 + z) * 2 + c

    sibling = owner(zh, xx, other)
    barrier = pltpu.get_barrier_semaphore()

    @pl.loop(0, NG - 1, unroll=31)
    def _(t):
        pl.semaphore_signal(barrier, inc=1, device_id={"ingest": ingest_peer(t)}, device_id_type=MESH)

    small = [
        pltpu.make_async_copy(a, b, lsem.at[8 + k])
        for k, (a, b) in enumerate(((asg_in, asg), (order_in, order), (dest_in, dest)))]
    for c in small:
        c.start()
    loads = [
        pltpu.make_async_copy(rot, r, lsem.at[0]),
        pltpu.make_async_copy(vec, x.at[pl.ds(0, BROWS)], lsem.at[1]),
    ]
    for k in range(4):
        loads.append(pltpu.make_async_copy(
            cen.at[pl.ds(pl.multiple_of(core * HALF, HALF), HALF)],
            x.at[pl.ds(BROWS + HALF * k, HALF)], lsem.at[2 + k]))
    for c in loads:
        c.start()

    @pl.loop(rank + 1, NI)
    def _(n):
        pl.semaphore_signal(
            barrier, inc=1, device_id={"index": owner(n >> 3, (n >> 1) & 3, n & 1)}, device_id_type=MESH)

    for c in small:
        c.wait()
    sub = lax.broadcasted_iota(i32, (32, 32), 0)
    lan = lax.broadcasted_iota(i32, (32, 32), 1)
    eye = sub == lan
    d_row = jnp.broadcast_to(dest[...], (32, 32))
    d_col = jnp.sum(jnp.where(eye, d_row, 0), axis=1, keepdims=True)
    o_col = jnp.sum(jnp.where(eye, jnp.broadcast_to(order[...], (32, 32)), 0), axis=1, keepdims=True)
    n_live = live[0]
    slot = jnp.sum(jnp.where((d_row == d_col) & (lan < sub) & (lan < n_live), 1, 0), axis=1, keepdims=True)
    k_col = lax.broadcasted_iota(i32, (32, 1), 0)
    target = jnp.where(k_col < n_live, d_col * CAP + slot, -1)
    q = lax.broadcasted_iota(i32, (32, 128), 1)
    blk = jnp.sum(jnp.where(target == q, o_col - NG, 0), axis=0, keepdims=True) + NG
    blkv[...] = jnp.broadcast_to(blk, (8, 128))
    to_smem = pltpu.make_async_copy(blkv, blks, lsem.at[6])
    to_smem.start()

    lane8 = lax.broadcasted_iota(i32, (8, 128), 1)
    sub8 = lax.broadcasted_iota(i32, (8, 128), 0)
    slot8 = lane8 >> 5
    low8 = lane8 & 31

    a = lanes(jnp.broadcast_to(asg[...], (8, 128)), (sub8 & 3) * 32 + low8)
    a_grp = ((a >> 5) & 1) * QUADS + (a >> 8)
    a_pos = ((a >> 6) & 3) * 32 + (a & 31)
    a_val = jnp.where(sub8 < 4, a_grp, a_pos).astype(f32)

    for c in loads:
        c.wait()
    y = jnp.dot(x[...], r[...], preferred_element_type=f32).astype(bf16).astype(f32)
    yt = y.T
    rt = yt[:, :BROWS].reshape(NG, OCT, 8, BROWS)
    tt = yt[:, BROWS:].reshape(NG, OCT, 8, BROWS)
    turn = ((slot8 - g) & 3)[None]
    tail = jnp.where(turn == 0, tt[:, 0], jnp.where(turn == 1, tt[:, 1], jnp.where(turn == 2, tt[:, 2], a_val[None])))
    sent_tail[...] = tail.astype(bf16)
    send[...] = rt.astype(bf16)

    pl.semaphore_wait(barrier, NG - 1 + rank)

    def scatter(k, src, dst):
        @pl.loop(0, NG - 1, unroll=31)
        def _(t):
            to = ingest_peer(t)
            pltpu.make_async_remote_copy(
                src_ref=src.at[to], dst_ref=dst.at[g], send_sem=s1.at[k], recv_sem=r1.at[k],
                device_id={"ingest": to}, device_id_type=MESH).start()

        return pltpu.make_async_remote_copy(
            src_ref=src.at[pl.ds(0, NG - 1)], dst_ref=dst.at[pl.ds(0, NG - 1)],
            send_sem=s1.at[k], recv_sem=r1.at[k],
            device_id={"ingest": (g + 1) & (NG - 1)}, device_id_type=MESH)

    @pl.when(core == 1)
    def _():
        pl.semaphore_signal(paired, inc=1, device_id={"index": sibling}, device_id_type=MESH)

    @pl.loop(0, rank)
    def _(n):
        pl.semaphore_signal(
            entered.at[zh], inc=1, device_id={"index": owner(n >> 3, (n >> 1) & 3, n & 1)}, device_id_type=MESH)

    tails = scatter(0, sent_tail, tail_in)
    features = scatter(1, send, recv)


    tail_in[pl.ds(g, 1)] = sent_tail[pl.ds(g, 1)]
    recv[pl.ds(g, 1)] = send[pl.ds(g, 1)]
    recv[NG] = jnp.zeros((OCT, 8, BROWS), bf16)
    looked[NG] = jnp.zeros((OCT, 8, BROWS), f32)
    to_smem.wait()

    tails.wait_recv()
    slips = []
    for quad in range(QUADS):
        m = [tail_in[quad * 4 + j].astype(f32) for j in range(4)]
        for f in range(4):
            t = m[3]
            for j in range(3):
                t = jnp.where(slot8 == (f + j) % 4, m[j], t)
            if f < OCT:
                tbl[core, quad, f] = t.astype(bf16)
        slips.append(t)

    def swap(half):
        return pltpu.make_async_remote_copy(
            src_ref=tbl.at[half], dst_ref=tbl.at[half], send_sem=swap_sem.at[0], recv_sem=swap_sem.at[1],
            device_id={"index": sibling}, device_id_type=MESH)

    @pl.when(core == 0)
    def _():
        pl.semaphore_wait(paired, 1)

    swap(core).start()

    for b in range(NG):
        v = lanes(slips[b // 4], 32 * ((3 + b) % 4) + low8)
        grp[b:b + 1] = jnp.sum(jnp.where(sub8 == slot8, v, 0.0), axis=0, keepdims=True).astype(i32)
        pos[b:b + 1] = jnp.sum(jnp.where(sub8 == slot8 + 4, v, 0.0), axis=0, keepdims=True).astype(i32)

    def look(half, first):
        table = [[tbl[half, quad, f].astype(f32) for f in range(OCT)] for quad in range(QUADS)]

        @pl.loop(0, NG, unroll=32)
        def _(b):
            lane0 = jnp.broadcast_to(pos[pl.ds(b, 1)], (8, 128))
            want = jnp.broadcast_to(grp[pl.ds(b, 1)], (8, 128)) - half * QUADS
            for f in range(OCT):
                idx = (lane0 + 32 * f) & 127
                acc = jnp.zeros((8, 128), f32) if first else looked[b, f]
                for quad in range(QUADS):
                    acc = jnp.where(want == quad, lanes(table[quad][f], idx), acc)
                looked[b, f] = acc

    look(core, True)
    swap(other).wait_recv()
    look(other, False)

    columns = pl.ds(pl.multiple_of(i * WIDE, WIDE), WIDE)

    def pack(p):
        for f in range(OCT):
            for s in range(CAP):
                b = blks[0, p * CAP + s]
                send2[p, f, :, s * BROWS:(s + 1) * BROWS] = (recv[b, f].astype(f32) - looked[b, f]).astype(bf16)

    def deliver(z, x_, c, sent):
        p = owner(z, x_, c)
        pack(p)
        pltpu.make_async_remote_copy(
            src_ref=send2.at[p], dst_ref=out.at[:, :, columns], send_sem=s2.at[sent], recv_sem=r2,
            device_id={"index": p}, device_id_type=MESH).start()

    features.wait_recv()

    def messages(n, sent):
        some = out.at[:, :, pl.ds(0, n * WIDE)]
        return pltpu.make_async_remote_copy(
            src_ref=some, dst_ref=some, send_sem=s2.at[sent], recv_sem=r2,
            device_id={"index": sibling}, device_id_type=MESH)

    def far(z, ahead):
        @pl.when(z > zh)
        def _():
            pl.semaphore_wait(entered.at[z], 8)

        @pl.loop(0, 8)
        def _(m):
            k = m >> 1
            x_ = (xx + jnp.where(k == 3, 0, jnp.where(k == 0, 2, 2 * k - 1))) & 3
            deliver(z, x_, core ^ (m & 1), jnp.where(m < ahead, 0, 1))

    step = 1 + jnp.where((zh == 1) | ((zh == 0) & ((g & 3) < FIRST)), 1, 0)
    z0 = zh + step
    z0 = jnp.where(z0 >= 3, z0 - 3, z0)
    far(z0, AHEAD)

    far(3 - zh - z0, 0)

    @pl.when(spot < 7)
    def _():
        pl.semaphore_wait(entered.at[zh], 7 - spot)

    @pl.loop(1, 8)
    def _(m):
        deliver(zh, (xx + (m >> 1)) & 3, core ^ (m & 1), 1)


    pack(i)
    own = pltpu.make_async_copy(send2.at[i], out.at[:, :, columns], lsem.at[7])
    own.start()
    tails.wait_send()
    features.wait_send()
    swap(core).wait_send()
    own.wait()

    messages(AHEAD, 0).wait_send()
    messages(NI - 1 - AHEAD, 1).wait_send()
    messages(NI - 1, 1).wait_recv()


def body(vectors, rotation, centroids, assignment, block_order, destination, live_count):
    bf16, f32, i32 = jnp.bfloat16, jnp.float32, jnp.int32
    hbm = pl.BlockSpec(memory_space=pltpu.HBM)
    smem = pl.BlockSpec(memory_space=pltpu.SMEM)
    dma = pltpu.SemaphoreType.DMA
    arrays = [
        pltpu.with_memory_space_constraint(a, pltpu.HBM)
        for a in (vectors, rotation, centroids, assignment.reshape(1, BROWS), block_order, destination.reshape(1, NG))]
    rebalanced = pl.pallas_call(
        kernel,
        out_shape=jax.ShapeDtypeStruct((OCT, 8, NI * WIDE), bf16),
        in_specs=[hbm] * 6 + [smem],
        out_specs=pl.BlockSpec(memory_space=pl.ANY),
        scratch_shapes=[
            pltpu.VMEM((1, BROWS), i32),
            pltpu.VMEM((1, NG), i32),
            pltpu.VMEM((1, NG), i32),
            pltpu.VMEM((2 * BROWS, D), bf16),
            pltpu.VMEM((D, D), bf16),
            pltpu.VMEM((NG, OCT, 8, BROWS), bf16),
            pltpu.VMEM((NG + 1, OCT, 8, BROWS), bf16),
            pltpu.VMEM((NG, 8, BROWS), bf16),
            pltpu.VMEM((NG, 8, BROWS), bf16),
            pltpu.VMEM((2, QUADS, OCT, 8, 128), bf16),
            pltpu.VMEM((NG, 128), i32),
            pltpu.VMEM((NG, 128), i32),
            pltpu.VMEM((NG + 1, OCT, 8, 128), f32),
            pltpu.VMEM((NI, OCT, 8, WIDE), bf16),
            pltpu.VMEM((8, 128), i32),
            pltpu.SMEM((8, 128), i32),
            dma((11,)), dma((2,)), dma((2,)), dma((2,)), dma((2,)), dma,
            pltpu.SemaphoreType.REGULAR((3,)), pltpu.SemaphoreType.REGULAR,
        ],
        compiler_params=pltpu.CompilerParams(
            collective_id=0, has_side_effects=True, vmem_limit_bytes=40 * 1024 * 1024),
        name="route",
    )(*arrays, live_count)
    return rebalanced.reshape(FEAT, NI * WIDE)


def solution(mesh):
    return jax.shard_map(
        body,
        mesh=mesh,
        in_specs=(
            P(("index", "ingest"), None),
            P(),
            P("ingest", None),
            P(("index", "ingest")),
            P("index", None),
            P("index", None, None),
            P("index"),
        ),
        out_specs=P("ingest", "index"),
        check_vma=False,
    )
```
